512 devices in a mesh: rad: 32 (over x_lo, y, core), ord: 16 (over z, x_hi).
Axes of the slice: x: 4 (x_hi: 2, x_lo: 2; x = x_hi * 2 + x_lo), y: 8, z: 8, core: 2. Of those that a mesh axis runs over, the one named last changes fastest.
Arguments:
- velocity: bfloat16 [6, 32, 133120], P(None, 'rad', 'ord'), may hold values from -0.5 to 0.5
- magnetic: bfloat16 [6, 32, 133120], P(None, 'rad', 'ord'), may hold values from -0.5 to 0.5
- legendre: bfloat16 [192, 133120], P('rad', 'ord'), may hold values from -1 to 1
- quad_weights: float32 [384], replicated, may hold values from 0.2 to 1.5
- orders: int32 [512], replicated, may hold values from 0 to 511, as said below
- offsets: int32 [512], P('ord'), may hold values from 0 to 8207, as said below
Outputs:
- motional: bfloat16 [6, 32, 133120], P(None, 'rad', 'ord')
- advected: bfloat16 [6, 32, 133120], P(None, 'rad', 'ord')
The draws below stay inside these ranges and needn't reach their ends.
Inputs may be any that keep to these rules, and one draw needn't show every extreme that they name: Every order appears in exactly one slot; the 32 slots of one ord index hold orders m and 511 - m in pairs. Within one ord index, slot s owns packed entries offsets[s] to offsets[s] + 512 - orders[s] - 1; these runs do not intersect, fill entries 0 to 8207 exactly, and the shortest run of each ord index comes last.
All inputs are finite; a program needn't handle non-finite values.
Results may differ from the reference program's by a relative error of at most 0.0081.
Values may be sent and summed in bfloat16 or wider, within the bound.
No kernel may reach another device: no remote copies, remote signals or barrier semaphores. Data moves between devices by JAX's collectives and lax.ppermute only.
A program may use at most 64 MiB of HBM per device.

```python
import math
import jax
import jax.numpy as jnp
from jax import lax

L = 512
NTH_HALF = 192
NPHI = 1536
M_DEV = 32
NR = 32
NTH = 384
PACK = 8320
PACK_ALL = 133120


def snake_layout(key):
    base = jax.random.fold_in(key, 11)
    pair_key, flip_key, place_key = jax.random.split(base, 3)
    groups = L // M_DEV
    half_count = M_DEV // 2
    pairs = jax.random.permutation(pair_key, L // 2).astype(jnp.int32).reshape(groups, half_count)
    flips = jax.random.randint(flip_key, (groups, half_count), 0, 2)
    first = jnp.where(flips == 1, L - 1 - pairs, pairs)
    second = L - 1 - first
    layout = jnp.stack([first, second], 2).reshape(groups, M_DEV).astype(jnp.int32)
    lengths = L - layout
    place_keys = jax.random.split(place_key, groups)
    placement = jax.vmap(lambda k: jax.random.permutation(k, M_DEV))(place_keys).astype(jnp.int32)
    shortest = jnp.argmin(lengths, axis=1).astype(jnp.int32)
    last_slot = placement[:, -1:]
    placement = jnp.where(placement == shortest[:, None], last_slot, placement)
    placement = placement.at[:, -1].set(shortest)
    placed = jnp.take_along_axis(lengths, placement, 1)
    starts = (jnp.cumsum(placed, 1) - placed).astype(jnp.int32)
    row_ids = jnp.arange(groups, dtype=jnp.int32)[:, None]
    offsets = jnp.zeros((groups, M_DEV), jnp.int32).at[row_ids, placement].set(starts)
    return (layout.reshape(L), offsets.reshape(L))


def draw_orders(key, part):
    layout, offsets = snake_layout(key)
    return layout


def draw_offsets(key, part):
    layout, offsets = snake_layout(key)
    return offsets


def shard_levels(stream_key, extent, cuts, least, largest):
    factor_of = 1.0
    for axis_at, blocks in cuts:
        steps = jax.random.uniform(jax.random.fold_in(jax.random.fold_in(stream_key, 6), axis_at), (blocks,), jnp.float32, least / len(cuts), largest / len(cuts))
        factor_of = factor_of * jnp.repeat(jnp.exp(steps), extent[axis_at] // blocks).reshape((-1,) + (1,) * (len(extent) - 1 - axis_at))
    return factor_of


def normal_values(rng, extent, scale, limit, pieces=(), kind=jnp.bfloat16):
    values = jax.random.normal(rng, extent, jnp.float32) * scale
    if len(pieces) > 0:
        values = shard_levels(rng, extent, pieces, -0.22, 0.18) * values
    return jnp.clip(values, min=-limit, max=limit).astype(kind)


def setup_inputs(seed: int = 0) -> dict:
    streams_of = jax.random.split(jax.random.key(seed), 7)
    return {
        "velocity": normal_values(streams_of[0], (6, NR, PACK_ALL), ((2 * L) ** -0.5), 0.5, ((1, 32), (2, 16))),
        "magnetic": normal_values(streams_of[1], (6, NR, PACK_ALL), ((2 * L) ** -0.5), 0.5, ((1, 32), (2, 16))),
        "legendre": normal_values(streams_of[2], (NTH_HALF, PACK_ALL), ((2.0 / L) ** 0.5), 1.0, ((0, 32), (1, 16))),
        "quad_weights": jnp.clip(jnp.exp(jax.random.uniform(streams_of[3], (NTH,), jnp.float32, math.log(0.2), math.log(1.5))), 0.2, 1.5),
        "orders": draw_orders(jax.random.fold_in(streams_of[6], 71), 0),
        "offsets": draw_offsets(jax.random.fold_in(streams_of[6], 71), 0),
    }


def wave_tables(orders, nphi):
    azimuth = jnp.arange(nphi, dtype=jnp.int32)
    phase_steps = (orders[:, None] * azimuth[None, :]) % nphi
    angles = phase_steps.astype(jnp.float32) * (2.0 * math.pi / nphi)
    factor = jnp.where(orders == 0, 1.0, 2.0).astype(jnp.float32)[:, None]
    inverse = jnp.stack([factor * jnp.cos(angles), -factor * jnp.sin(angles)], 1).astype(jnp.bfloat16)
    norm_scale = nphi ** -0.5
    forward = jnp.stack([norm_scale * jnp.cos(angles), -norm_scale * jnp.sin(angles)], 2)
    forward = jnp.transpose(forward, (1, 0, 2)).astype(jnp.bfloat16)
    return inverse, forward


def reference(velocity, magnetic, legendre, quad_weights, orders, offsets):
    shell_total = magnetic.shape[1]
    rimmed = jnp.pad(magnetic.astype(jnp.float32), ((0, 0), (1, 1), (0, 0)))
    dmag = ((rimmed[:, 2:] - rimmed[:, :-2]) * 0.5).astype(jnp.bfloat16)
    spectral = jnp.concatenate([velocity, magnetic, dmag], 0)
    packed_len = spectral.shape[2]
    slot_ids = jnp.arange(L, dtype=jnp.int32)
    starts = (slot_ids // M_DEV) * PACK + offsets
    degree = jnp.arange(L, dtype=jnp.int32)
    positions = starts[:, None] + degree[None, :]
    inside_run = degree[None, :] < (L - orders)[:, None]
    parity = jnp.where(degree % 2 == 0, 1.0, -1.0).astype(jnp.float32)
    padded_table = jnp.pad(legendre, ((0, 0), (0, L)))
    order_tiles = jax.vmap(lambda first: lax.dynamic_slice_in_dim(padded_table, first, L, 1))(starts)
    tiles_wide = order_tiles.astype(jnp.float32)
    inverse, forward = wave_tables(orders, NPHI)
    weights = jnp.stack([quad_weights[:NTH_HALF], quad_weights[::-1][:NTH_HALF]], 0)
    spectral_pad = jnp.pad(jnp.moveaxis(spectral, 2, 0), ((0, L), (0, 0), (0, 0)))

    def one_shell(level):
        column = lax.dynamic_index_in_dim(spectral_pad, level, 2, keepdims=False)
        dense_coef = jnp.where(inside_run[:, :, None], column[positions], 0.0).astype(jnp.float32)
        signed_pair = jnp.stack([dense_coef, dense_coef * parity[None, :, None]], 2)
        grid = jnp.einsum("stj,sjhq->shtq", tiles_wide, signed_pair).astype(jnp.bfloat16)
        columns = grid.reshape(L, 2, NTH_HALF, 3, 3, 2).astype(jnp.float32)
        physical = jnp.einsum("shtfcr,srp->fchtp", columns, inverse.astype(jnp.float32))
        flow_grid, field_grid, slope_grid = physical[0], physical[1], physical[2]
        motional = jnp.stack([
            flow_grid[1] * field_grid[2] - flow_grid[2] * field_grid[1],
            flow_grid[2] * field_grid[0] - flow_grid[0] * field_grid[2],
            flow_grid[0] * field_grid[1] - flow_grid[1] * field_grid[0]], 0)
        advected = flow_grid[0][None] * slope_grid
        products = jnp.concatenate([motional, advected], 0).astype(jnp.bfloat16)
        harmonic = jnp.einsum("khtp,psr->khtsr", products.astype(jnp.float32), forward.astype(jnp.float32))
        harmonic = (harmonic * weights[None, :, :, None, None]).astype(jnp.bfloat16)
        summed = jnp.einsum("stj,khtsr->sjhkr", tiles_wide, harmonic.astype(jnp.float32))
        merged = summed[:, :, 0] + parity[None, :, None, None] * summed[:, :, 1]
        merged = jnp.where(inside_run[:, :, None, None], merged, 0.0).astype(jnp.bfloat16)
        targets = jnp.where(inside_run, positions, packed_len + L)
        result = jnp.zeros((packed_len, 6, 2), jnp.bfloat16).at[targets].set(merged, mode="drop")
        return result.reshape(packed_len, 12)

    result = lax.map(one_shell, jnp.arange(shell_total, dtype=jnp.int32))
    result = jnp.moveaxis(result, 2, 0)
    return result[:6], result[6:]
```

```python
import math

import jax
import jax.numpy as jnp
import ml_dtypes
import numpy as np
from jax import lax
from jax.experimental import pallas as pl
from jax.experimental.pallas import tpu as pltpu
from jax.sharding import Mesh
from jax.sharding import PartitionSpec as P

L = 512
NTH_HALF = 192
NPHI = 1536
PACK = 8320
SLOTS = 32
WIN = 640
HALF = 4096
WIDE = PACK - HALF
RAD = ("xl", "y", "c")
ORD = ("z", "xh")
SWAP = ("xh", "z")
BANDS = 8
ROWS = 24
UNROLL = 32
VMEM_LIMIT = 24 * 1024 * 1024
F32 = jnp.float32
BF16 = jnp.bfloat16


def vmem():
    return pl.BlockSpec(memory_space=pltpu.VMEM)


def smem():
    return pl.BlockSpec(memory_space=pltpu.SMEM)


def anywhere():
    return pl.BlockSpec(memory_space=pl.ANY)


def params():
    return pltpu.CompilerParams(vmem_limit_bytes=VMEM_LIMIT)


def canonical_table():
    m = np.arange(L)[:, None]
    p = np.arange(NPHI)[None, :]
    angles = (m * p % NPHI).astype(np.float64) * (2.0 * math.pi / NPHI)
    factor = np.where(m == 0, 1.0, 2.0)
    table = np.concatenate([factor * np.cos(angles), -factor * np.sin(angles)], 0)
    return table.astype(np.float32).astype(ml_dtypes.bfloat16)


def band_rows(band):
    return (16 * band, 16 * band + 8, 128 + 8 * band, 192 + 8 * band)


def slot_window(off_ref, len_ref, s):
    start = off_ref[s]
    base = jnp.minimum((start // 128) * 128, PACK - WIN)
    base = pl.multiple_of(base, 128)
    return start, len_ref[s], base


def synthesis_kernel(off_ref, len_ref, spec_ref, same_ref, near_ref, far_ref, *refs):
    out_ref, coef_ref, acc_a, acc_b = refs
    lane = lax.broadcasted_iota(jnp.int32, (ROWS, WIN), 1)

    def mask_slot(s, carry):
        start, count, base = slot_window(off_ref, len_ref, s)
        degree = lane + (base - start)
        inside = (degree >= 0) & (degree < count)
        even = (degree & 1) == 0
        coef = jnp.where(inside, spec_ref[:, pl.ds(base, WIN)].astype(F32), 0.0)
        pair = jnp.concatenate([jnp.where(even, coef, 0.0), jnp.where(even, 0.0, coef)], 0)
        coef_ref[s] = pair.astype(BF16)
        return carry

    lax.fori_loop(0, SLOTS, mask_slot, 0, unroll=4)
    def one_slot(s, carry):
        start, count, base = slot_window(off_ref, len_ref, s)
        coef = coef_ref[s]
        both = jnp.concatenate(
            [
                lax.dot_general(
                    coef,
                    part[:, pl.ds(base, WIN)],
                    (((1,), (1,)), ((), ())),
                    preferred_element_type=F32,
                )
                for part in (same_ref, near_ref, far_ref)
            ],
            1,
        )
        north = both[:ROWS] + both[ROWS:]
        south = both[:ROWS] - both[ROWS:]
        acc_a[pl.ds(s, 24, stride=32), :] = north[:, 0:128]
        acc_b[pl.ds(s, 24, stride=32), :] = north[:, 128:256]
        acc_a[pl.ds(768 + s, 24, stride=32), :] = south[:, 0:128]
        acc_b[pl.ds(768 + s, 24, stride=32), :] = south[:, 128:256]
        return carry

    lax.fori_loop(0, SLOTS, one_slot, 0, unroll=UNROLL)
    for hemi in range(2):
        held = slice(768 * hemi, 768 * hemi + 640)
        turned = jnp.transpose(jnp.concatenate([acc_a[held], acc_b[held]], 1))
        for band in range(BANDS):
            rows = jnp.concatenate([turned[at : at + 6] for at in band_rows(band)], 0)
            out_ref[hemi * BANDS + band] = rows.astype(BF16)


def synthesis(offsets, lengths, spec, same, near, far):
    return pl.pallas_call(
        synthesis_kernel,
        out_shape=jax.ShapeDtypeStruct((16, ROWS, 640), BF16),
        in_specs=[smem(), smem(), vmem(), vmem(), vmem(), vmem()],
        out_specs=vmem(),
        scratch_shapes=[
            pltpu.VMEM((SLOTS, 2 * ROWS, WIN), BF16),
            pltpu.VMEM((1536, 128), F32),
            pltpu.VMEM((1536, 128), F32),
        ],
        compiler_params=params(),
        name="synthesis",
    )(offsets, lengths, spec, same, near, far)


def join_halves(first, second, half):
    low = lax.broadcasted_iota(jnp.int32, first.shape, 1) < 64
    if half == 0:
        return jnp.where(low, first, pltpu.roll(second, 64, 1))
    return jnp.where(low, pltpu.roll(first, 64, 1), second)


def waves_kernel(source_ref, table_ref, after_ref, out_ref):
    column = lax.broadcasted_iota(jnp.int32, (2 * L, 2 * L), 1)
    chosen = jnp.where(column == source_ref[...], 1.0, 0.0).astype(BF16)
    step = 512
    for at in range(0, NPHI, step):
        out_ref[:, at : at + step] = jnp.dot(
            chosen, table_ref[:, at : at + step], preferred_element_type=F32
        ).astype(BF16)


def wave_rows(source, table, after):
    return pl.pallas_call(
        waves_kernel,
        out_shape=jax.ShapeDtypeStruct((2 * L, NPHI), BF16),
        in_specs=[vmem(), vmem(), anywhere()],
        out_specs=vmem(),
        compiler_params=params(),
        cost_estimate=pl.CostEstimate(
            flops=8 * L * L * NPHI, bytes_accessed=8 * L * NPHI, transcendentals=0
        ),
        name="waves",
    )(source, table, after)


def azimuth_kernel(g_ref, t_ref, row_ref, lane_ref, out_ref, a_ref, h_ref):
    for c in range(9):
        tile = slice(128 * (c // 2), 128 * (c // 2) + 128)
        for pair in range(8):
            first = g_ref[2 * pair][:, tile].astype(F32)
            second = g_ref[2 * pair + 1][:, tile].astype(F32)
            a_ref[ROWS * c : ROWS * (c + 1), 128 * pair : 128 * (pair + 1)] = join_halves(
                first, second, c % 2
            )
    values = a_ref[...].astype(BF16)
    step = 512
    for chunk in range(NPHI // step):
        waves = t_ref[:, step * chunk : step * (chunk + 1)]
        grid = jnp.dot(values, waves, preferred_element_type=F32)
        u = [grid[ROWS * c : ROWS * (c + 1)] for c in range(3)]
        b = [grid[ROWS * (3 + c) : ROWS * (4 + c)] for c in range(3)]
        d = [grid[ROWS * (6 + c) : ROWS * (7 + c)] for c in range(3)]
        products = jnp.concatenate(
            [
                u[1] * b[2] - u[2] * b[1],
                u[2] * b[0] - u[0] * b[2],
                u[0] * b[1] - u[1] * b[0],
                u[0] * d[0],
                u[0] * d[1],
                u[0] * d[2],
            ],
            0,
        ).astype(BF16)
        part = lax.dot_general(
            products, waves, (((1,), (1,)), ((), ())), preferred_element_type=F32
        )
        if chunk == 0:
            h_ref[...] = part
        else:
            h_ref[...] += part
    h_ref[...] = h_ref[...] * row_ref[...] * lane_ref[...]
    for dest in range(16):
        tile = slice(128 * (dest // 2), 128 * (dest // 2) + 128)
        parts = []
        for k in range(0, 6, 2):
            first = h_ref[ROWS * k : ROWS * (k + 1), tile]
            second = h_ref[ROWS * (k + 1) : ROWS * (k + 2), tile]
            parts.append(join_halves(first, second, dest % 2))
        out_ref[dest] = jnp.concatenate(parts, 1).astype(BF16)


def azimuth(grid, waves, row_scale, lane_scale):
    return pl.pallas_call(
        azimuth_kernel,
        out_shape=jax.ShapeDtypeStruct((16, ROWS, 384), BF16),
        in_specs=[vmem()] * 4,
        out_specs=vmem(),
        scratch_shapes=[pltpu.VMEM((216, 1024), F32), pltpu.VMEM((144, 1024), F32)],
        compiler_params=params(),
        name="azimuth",
    )(grid, waves, row_scale, lane_scale)


def analysis_kernel(off_ref, len_ref, r_ref, same_ref, near_ref, far_ref, mot_ref, adv_ref, *refs):
    wide, turned_a, turned_b, out = refs
    gap = jnp.zeros((2, 384), F32)
    for hemi in range(2):
        for band in range(BANDS):
            held = r_ref[hemi * BANDS + band].astype(F32)
            for i, at in enumerate(band_rows(band)):
                wide[at : at + 8, :] = jnp.concatenate([held[6 * i : 6 * i + 6], gap], 0)
        flip = jnp.transpose(wide[...])
        at = 512 * hemi
        for turned, lanes in ((turned_a, slice(0, 128)), (turned_b, slice(128, 256))):
            turned[at : at + 192] = flip[0:192, lanes]
            turned[at + 192 : at + 256] = jnp.zeros((64, 128), F32)
            turned[at + 256 : at + 448] = flip[192:384, lanes]
            turned[at + 448 : at + 512] = jnp.zeros((64, 128), F32)
    out[...] = jnp.zeros_like(out)
    lane = lax.broadcasted_iota(jnp.int32, (16, WIN), 1)

    def one_slot(s, carry):
        start, count, base = slot_window(off_ref, len_ref, s)
        degree = lane + (base - start)
        inside = (degree >= 0) & (degree < count)
        even = (degree & 1) == 0
        rows_a = turned_a[pl.ds(s, 32, stride=32), :].astype(BF16)
        rows_b = turned_b[pl.ds(s, 32, stride=32), :].astype(BF16)
        window = pl.ds(base, WIN)
        both = jnp.dot(rows_a, same_ref[:, window], preferred_element_type=F32)
        rest = jnp.concatenate([near_ref[:, window], far_ref[:, window]], 0)
        both += jnp.dot(rows_b, rest, preferred_element_type=F32)
        merged = both[:16] + jnp.where(even, both[16:], -both[16:])
        held = out[:, pl.ds(base, WIN)]
        out[:, pl.ds(base, WIN)] = jnp.where(inside, merged, held)
        return carry

    lax.fori_loop(0, SLOTS, one_slot, 0, unroll=UNROLL)
    mot_ref[...] = out[0:6].astype(BF16)
    adv_ref[...] = out[8:14].astype(BF16)


def analysis(offsets, lengths, spectra, same, near, far):
    shape = jax.ShapeDtypeStruct((6, PACK), BF16)
    return pl.pallas_call(
        analysis_kernel,
        out_shape=(shape, shape),
        in_specs=[smem(), smem(), vmem(), vmem(), vmem(), vmem()],
        out_specs=(vmem(), vmem()),
        scratch_shapes=[
            pltpu.VMEM((256, 384), F32),
            pltpu.VMEM((1024, 128), F32),
            pltpu.VMEM((1024, 128), F32),
            pltpu.VMEM((16, PACK), F32),
        ],
        compiler_params=params(),
        name="analysis",
    )(offsets, lengths, spectra, same, near, far)


def entry_kernel(p_ref, padded_ref, p_out):
    rows = p_ref[...].astype(F32)
    padded_ref[...] = jnp.concatenate([rows, jnp.zeros((2, PACK), F32)], 0).astype(BF16)
    p_out[...] = p_ref[...]


def entry(legendre):
    return pl.pallas_call(
        entry_kernel,
        out_shape=(
            jax.ShapeDtypeStruct((8, PACK), BF16),
            jax.ShapeDtypeStruct((6, PACK), BF16),
        ),
        in_specs=[vmem()],
        out_specs=(vmem(),) * 2,
        compiler_params=params(),
        name="entry",
    )(legendre)


def hold_kernel(x_ref, after_ref, out_ref):
    out_ref[...] = x_ref[...]


def hold(x, after):
    return pl.pallas_call(
        hold_kernel,
        out_shape=jax.ShapeDtypeStruct(x.shape, x.dtype),
        in_specs=[vmem(), anywhere()],
        out_specs=vmem(),
        compiler_params=params(),
        name="hold",
    )(x, after)


def gathered_table(legendre):
    padded, legendre = entry(legendre)
    same = lax.all_gather(padded, ("y", "c"), axis=0, tiled=True)
    other = lax.ppermute(legendre, "xl", [(0, 1), (1, 0)])
    near = lax.all_gather(other, "y", axis=0)
    near = jnp.pad(near, ((0, 0), (0, 2), (0, 0))).reshape(64, PACK)
    far = lax.ppermute(near, "c", [(0, 1), (1, 0)])
    return same, near, far


def radial_slope(magnetic, after):
    count = lax.axis_size(RAD)
    links = [(i, i + 1) for i in range(1, count - 1, 2)]
    magnetic = hold(magnetic, after)
    swapped = lax.ppermute(magnetic, "c", [(0, 1), (1, 0)])
    linked = lax.ppermute(magnetic, RAD, links + [(j, i) for i, j in links])
    swapped, linked = swapped.astype(F32), linked.astype(F32)
    first = lax.axis_index("c") == 0
    slope = jnp.where(first, swapped - linked, linked - swapped)
    return (slope * 0.5).astype(BF16)


def table_weights(quad_weights):
    row = jnp.arange(6 * ROWS, dtype=jnp.int32) % ROWS
    run = row // 6
    column = lax.axis_index("xl")
    core = lax.axis_index("c")
    column = jnp.where(run < 2, column, 1 - column)
    core = jnp.where(run < 2, run, jnp.where(run == 2, core, 1 - core))
    theta = ((column * 8 + lax.axis_index("z")) * 2 + core) * 6 + row % 6
    theta = jnp.where(lax.axis_index("xh") == 0, theta, 2 * NTH_HALF - 1 - theta)
    chosen = theta[:, None] == jnp.arange(2 * NTH_HALF, dtype=jnp.int32)[None, :]
    return jnp.sum(jnp.where(chosen, quad_weights[None, :], 0.0), 1, keepdims=True)


def shards(velocity, magnetic, legendre, quad_weights, orders, offsets):
    velocity = velocity.reshape(6, PACK)
    magnetic = magnetic.reshape(6, PACK)
    ord_index = lax.axis_index(ORD)
    local_orders = lax.dynamic_slice_in_dim(orders, ord_index * SLOTS, SLOTS)
    lengths = L - local_orders
    same, near, far = gathered_table(legendre)
    slope = radial_slope(magnetic, near)
    spec = jnp.concatenate([velocity, magnetic, slope, jnp.zeros_like(velocity)], 0)

    swapped = jnp.transpose(orders.reshape(8, 2, SLOTS), (1, 0, 2)).reshape(L)
    source = swapped.reshape(16, 1, SLOTS) + jnp.array([0, L], jnp.int32)[None, :, None]
    unscale = jnp.where(swapped == 0, 1.0, 0.5).astype(F32).reshape(16, 1, SLOTS)
    lane_scale = jnp.broadcast_to(unscale, (16, 2, SLOTS)).reshape(1, 2 * L)
    row_scale = table_weights(quad_weights) * (NPHI ** (-0.5))
    grid = synthesis(offsets, lengths, spec, same, near, far)
    waves = wave_rows(source.reshape(2 * L, 1), jnp.asarray(canonical_table()), grid)
    grid = lax.all_to_all(grid, SWAP, 0, 0)
    harmonic = azimuth(grid, waves, row_scale, lane_scale)
    spectra = lax.all_to_all(harmonic, SWAP, 0, 0)
    motional, advected = analysis(offsets, lengths, spectra, same, near, far)
    return motional.reshape(6, 1, PACK), advected.reshape(6, 1, PACK)


def solution(mesh):
    fine = Mesh(mesh.devices.reshape(2, 8, 2, 8, 2), RAD + ORD)
    return jax.shard_map(
        shards,
        mesh=fine,
        in_specs=(
            P(None, RAD, ORD),
            P(None, RAD, ORD),
            P(RAD, ORD),
            P(),
            P(),
            P(ORD),
        ),
        out_specs=(P(None, RAD, ORD), P(None, RAD, ORD)),
        check_vma=False,
    )
```

```python
import math

import jax
import jax.numpy as jnp
import ml_dtypes
import numpy as np
from jax import lax
from jax.experimental import pallas as pl
from jax.experimental.pallas import tpu as pltpu
from jax.sharding import Mesh
from jax.sharding import PartitionSpec as P

L = 512
NTH_HALF = 192
NPHI = 1536
PACK = 8320
SLOTS = 32
WIN = 640
HALF = 4096
WIDE = PACK - HALF
RAD = ("xl", "y", "c")
ORD = ("z", "xh")
SWAP = ("xh", "z")
BANDS = 8
ROWS = 24
UNROLL = 32
VMEM_LIMIT = 24 * 1024 * 1024
F32 = jnp.float32
BF16 = jnp.bfloat16


def vmem():
    return pl.BlockSpec(memory_space=pltpu.VMEM)


def smem():
    return pl.BlockSpec(memory_space=pltpu.SMEM)


def anywhere():
    return pl.BlockSpec(memory_space=pl.ANY)


def params():
    return pltpu.CompilerParams(vmem_limit_bytes=VMEM_LIMIT)


def canonical_table():
    m = np.arange(L)[:, None]
    p = np.arange(NPHI)[None, :]
    angles = (m * p % NPHI).astype(np.float64) * (2.0 * math.pi / NPHI)
    factor = np.where(m == 0, 1.0, 2.0)
    table = np.concatenate([factor * np.cos(angles), -factor * np.sin(angles)], 0)
    return table.astype(np.float32).astype(ml_dtypes.bfloat16)


def band_rows(band):
    return (16 * band, 16 * band + 8, 128 + 8 * band, 192 + 8 * band)


def slot_window(off_ref, len_ref, s):
    start = off_ref[s]
    base = jnp.minimum((start // 128) * 128, PACK - WIN)
    base = pl.multiple_of(base, 128)
    return start, len_ref[s], base


def synthesis_kernel(off_ref, len_ref, spec_ref, same_ref, near_ref, far_ref, *refs):
    out_ref, coef_ref, acc_a, acc_b = refs
    lane = lax.broadcasted_iota(jnp.int32, (ROWS, WIN), 1)

    def mask_slot(s, carry):
        start, count, base = slot_window(off_ref, len_ref, s)
        degree = lane + (base - start)
        inside = (degree >= 0) & (degree < count)
        even = (degree & 1) == 0
        coef = jnp.where(inside, spec_ref[:, pl.ds(base, WIN)].astype(F32), 0.0)
        pair = jnp.concatenate([jnp.where(even, coef, 0.0), jnp.where(even, 0.0, coef)], 0)
        coef_ref[s] = pair.astype(BF16)
        return carry

    lax.fori_loop(0, SLOTS, mask_slot, 0, unroll=4)
    def one_slot(s, carry):
        start, count, base = slot_window(off_ref, len_ref, s)
        coef = coef_ref[s]
        both = jnp.concatenate(
            [
                lax.dot_general(
                    coef,
                    part[:rows, pl.ds(base, WIN)],
                    (((1,), (1,)), ((), ())),
                    preferred_element_type=F32,
                )
                for part, rows in ((same_ref, 128), (near_ref, 64), (far_ref, 64))
            ],
            1,
        )
        north = both[:ROWS] + both[ROWS:]
        south = both[:ROWS] - both[ROWS:]
        acc_a[pl.ds(s, 24, stride=32), :] = north[:, 0:128]
        acc_b[pl.ds(s, 24, stride=32), :] = north[:, 128:256]
        acc_a[pl.ds(768 + s, 24, stride=32), :] = south[:, 0:128]
        acc_b[pl.ds(768 + s, 24, stride=32), :] = south[:, 128:256]
        return carry

    lax.fori_loop(0, SLOTS, one_slot, 0, unroll=UNROLL)
    for hemi in range(2):
        held = slice(768 * hemi, 768 * hemi + 640)
        turned = jnp.transpose(jnp.concatenate([acc_a[held], acc_b[held]], 1))
        for band in range(BANDS):
            rows = jnp.concatenate([turned[at : at + 6] for at in band_rows(band)], 0)
            out_ref[hemi * BANDS + band] = rows.astype(BF16)


def synthesis(offsets, lengths, spec, same, near, far):
    return pl.pallas_call(
        synthesis_kernel,
        out_shape=jax.ShapeDtypeStruct((16, ROWS, 640), BF16),
        in_specs=[smem(), smem(), vmem(), vmem(), vmem(), vmem()],
        out_specs=vmem(),
        scratch_shapes=[
            pltpu.VMEM((SLOTS, 2 * ROWS, WIN), BF16),
            pltpu.VMEM((1536, 128), F32),
            pltpu.VMEM((1536, 128), F32),
        ],
        compiler_params=params(),
        name="synthesis",
    )(offsets, lengths, spec, same, near, far)


def join_halves(first, second, half):
    low = lax.broadcasted_iota(jnp.int32, first.shape, 1) < 64
    if half == 0:
        return jnp.where(low, first, pltpu.roll(second, 64, 1))
    return jnp.where(low, pltpu.roll(first, 64, 1), second)


def waves_kernel(source_ref, table_ref, out_ref):
    column = lax.broadcasted_iota(jnp.int32, (2 * L, 2 * L), 1)
    chosen = jnp.where(column == source_ref[...], 1.0, 0.0).astype(BF16)
    step = 512
    for at in range(0, NPHI, step):
        out_ref[:, at : at + step] = jnp.dot(
            chosen, table_ref[:, at : at + step], preferred_element_type=F32
        ).astype(BF16)


def wave_rows(source, table):
    return pl.pallas_call(
        waves_kernel,
        out_shape=jax.ShapeDtypeStruct((2 * L, NPHI), BF16),
        in_specs=[vmem(), vmem()],
        out_specs=vmem(),
        compiler_params=params(),
        cost_estimate=pl.CostEstimate(
            flops=8 * L * L * NPHI, bytes_accessed=8 * L * NPHI, transcendentals=0
        ),
        name="waves",
    )(source, table)


def azimuth_kernel(g_ref, t_ref, row_ref, lane_ref, out_ref, a_ref, h_ref):
    for c in range(9):
        tile = slice(128 * (c // 2), 128 * (c // 2) + 128)
        for pair in range(8):
            first = g_ref[2 * pair][:, tile].astype(F32)
            second = g_ref[2 * pair + 1][:, tile].astype(F32)
            a_ref[ROWS * c : ROWS * (c + 1), 128 * pair : 128 * (pair + 1)] = join_halves(
                first, second, c % 2
            )
    values = a_ref[...].astype(BF16)
    step = 512
    for chunk in range(NPHI // step):
        waves = t_ref[:, step * chunk : step * (chunk + 1)]
        grid = jnp.dot(values, waves, preferred_element_type=F32)
        u = [grid[ROWS * c : ROWS * (c + 1)] for c in range(3)]
        b = [grid[ROWS * (3 + c) : ROWS * (4 + c)] for c in range(3)]
        d = [grid[ROWS * (6 + c) : ROWS * (7 + c)] for c in range(3)]
        products = jnp.concatenate(
            [
                u[1] * b[2] - u[2] * b[1],
                u[2] * b[0] - u[0] * b[2],
                u[0] * b[1] - u[1] * b[0],
                u[0] * d[0],
                u[0] * d[1],
                u[0] * d[2],
            ],
            0,
        ).astype(BF16)
        part = lax.dot_general(
            products, waves, (((1,), (1,)), ((), ())), preferred_element_type=F32
        )
        if chunk == 0:
            h_ref[...] = part
        else:
            h_ref[...] += part
    h_ref[...] = h_ref[...] * row_ref[...] * lane_ref[...]
    for dest in range(16):
        tile = slice(128 * (dest // 2), 128 * (dest // 2) + 128)
        parts = []
        for k in range(0, 6, 2):
            first = h_ref[ROWS * k : ROWS * (k + 1), tile]
            second = h_ref[ROWS * (k + 1) : ROWS * (k + 2), tile]
            parts.append(join_halves(first, second, dest % 2))
        out_ref[dest] = jnp.concatenate(parts, 1).astype(BF16)


def azimuth(grid, waves, row_scale, lane_scale):
    return pl.pallas_call(
        azimuth_kernel,
        out_shape=jax.ShapeDtypeStruct((16, ROWS, 384), BF16),
        in_specs=[vmem()] * 4,
        out_specs=vmem(),
        scratch_shapes=[pltpu.VMEM((216, 1024), F32), pltpu.VMEM((144, 1024), F32)],
        compiler_params=params(),
        name="azimuth",
    )(grid, waves, row_scale, lane_scale)


def analysis_kernel(off_ref, len_ref, r_ref, same_ref, near_ref, far_ref, mot_ref, adv_ref, *refs):
    wide, turned_a, turned_b, out = refs
    gap = jnp.zeros((2, 384), F32)
    for hemi in range(2):
        for band in range(BANDS):
            held = r_ref[hemi * BANDS + band].astype(F32)
            for i, at in enumerate(band_rows(band)):
                wide[at : at + 8, :] = jnp.concatenate([held[6 * i : 6 * i + 6], gap], 0)
        flip = jnp.transpose(wide[...])
        at = 512 * hemi
        for turned, lanes in ((turned_a, slice(0, 128)), (turned_b, slice(128, 256))):
            turned[at : at + 192] = flip[0:192, lanes]
            turned[at + 192 : at + 256] = jnp.zeros((64, 128), F32)
            turned[at + 256 : at + 448] = flip[192:384, lanes]
            turned[at + 448 : at + 512] = jnp.zeros((64, 128), F32)
    out[...] = jnp.zeros_like(out)
    lane = lax.broadcasted_iota(jnp.int32, (16, WIN), 1)

    def one_slot(s, carry):
        start, count, base = slot_window(off_ref, len_ref, s)
        degree = lane + (base - start)
        inside = (degree >= 0) & (degree < count)
        even = (degree & 1) == 0
        rows_a = turned_a[pl.ds(s, 32, stride=32), :].astype(BF16)
        rows_b = turned_b[pl.ds(s, 32, stride=32), :].astype(BF16)
        window = pl.ds(base, WIN)
        both = jnp.dot(rows_a, same_ref[:, window], preferred_element_type=F32)
        rest = jnp.concatenate([near_ref[:64, window], far_ref[:64, window]], 0)
        both += jnp.dot(rows_b, rest, preferred_element_type=F32)
        merged = both[:16] + jnp.where(even, both[16:], -both[16:])
        held = out[:, pl.ds(base, WIN)]
        out[:, pl.ds(base, WIN)] = jnp.where(inside, merged, held)
        return carry

    lax.fori_loop(0, SLOTS, one_slot, 0, unroll=UNROLL)
    mot_ref[...] = out[0:6].astype(BF16)
    adv_ref[...] = out[8:14].astype(BF16)


def analysis(offsets, lengths, spectra, same, near, far):
    shape = jax.ShapeDtypeStruct((6, PACK), BF16)
    return pl.pallas_call(
        analysis_kernel,
        out_shape=(shape, shape),
        in_specs=[smem(), smem(), vmem(), vmem(), vmem(), vmem()],
        out_specs=(vmem(), vmem()),
        scratch_shapes=[
            pltpu.VMEM((256, 384), F32),
            pltpu.VMEM((1024, 128), F32),
            pltpu.VMEM((1024, 128), F32),
            pltpu.VMEM((16, PACK), F32),
        ],
        compiler_params=params(),
        name="analysis",
    )(offsets, lengths, spectra, same, near, far)


def entry_kernel(p_ref, padded_ref, p_out):
    rows = p_ref[...].astype(F32)
    padded_ref[...] = jnp.concatenate([rows, jnp.zeros((2, PACK), F32)], 0).astype(BF16)
    p_out[...] = p_ref[...]


def entry(legendre):
    return pl.pallas_call(
        entry_kernel,
        out_shape=(
            jax.ShapeDtypeStruct((8, PACK), BF16),
            jax.ShapeDtypeStruct((6, PACK), BF16),
        ),
        in_specs=[vmem()],
        out_specs=(vmem(),) * 2,
        compiler_params=params(),
        name="entry",
    )(legendre)


def hold_kernel(x_ref, *refs):
    refs[-1][...] = x_ref[...]


def hold(x, *after):
    return pl.pallas_call(
        hold_kernel,
        out_shape=jax.ShapeDtypeStruct(x.shape, x.dtype),
        in_specs=[vmem()] + [anywhere()] * len(after),
        out_specs=vmem(),
        compiler_params=params(),
        name="hold",
    )(x, *after)


def gathered_table(legendre, magnetic, *before):
    padded, legendre = entry(legendre)
    same = lax.all_gather(padded, ("y", "c"), axis=0, tiled=True)
    other = lax.ppermute(legendre, "xl", [(0, 1), (1, 0)])
    near = jnp.concatenate([lax.all_gather(hold(other, *before), "y", axis=0), magnetic[None]], 0)
    near = jnp.pad(near, ((0, 0), (0, 2), (0, 0))).reshape(72, PACK)
    far = lax.ppermute(near, "c", [(0, 1), (1, 0)])
    return same, near, far


def radial_slope(magnetic, far, *after):
    count = lax.axis_size(RAD)
    links = [(i, i + 1) for i in range(1, count - 1, 2)]
    linked = lax.ppermute(hold(magnetic, *after), RAD, links + [(j, i) for i, j in links])
    swapped, linked = far[64:70].astype(F32), linked.astype(F32)
    first = lax.axis_index("c") == 0
    slope = jnp.where(first, swapped - linked, linked - swapped)
    return (slope * 0.5).astype(BF16)


def table_weights(quad_weights):
    row = jnp.arange(6 * ROWS, dtype=jnp.int32) % ROWS
    run = row // 6
    column = lax.axis_index("xl")
    core = lax.axis_index("c")
    column = jnp.where(run < 2, column, 1 - column)
    core = jnp.where(run < 2, run, jnp.where(run == 2, core, 1 - core))
    theta = ((column * 8 + lax.axis_index("z")) * 2 + core) * 6 + row % 6
    theta = jnp.where(lax.axis_index("xh") == 0, theta, 2 * NTH_HALF - 1 - theta)
    chosen = theta[:, None] == jnp.arange(2 * NTH_HALF, dtype=jnp.int32)[None, :]
    return jnp.sum(jnp.where(chosen, quad_weights[None, :], 0.0), 1, keepdims=True)


def shards(velocity, magnetic, legendre, quad_weights, orders, offsets):
    velocity = velocity.reshape(6, PACK)
    magnetic = magnetic.reshape(6, PACK)
    ord_index = lax.axis_index(ORD)
    local_orders = lax.dynamic_slice_in_dim(orders, ord_index * SLOTS, SLOTS)
    lengths = L - local_orders
    swapped = jnp.transpose(orders.reshape(8, 2, SLOTS), (1, 0, 2)).reshape(L)
    source = swapped.reshape(16, 1, SLOTS) + jnp.array([0, L], jnp.int32)[None, :, None]
    unscale = jnp.where(swapped == 0, 1.0, 0.5).astype(F32).reshape(16, 1, SLOTS)
    lane_scale = jnp.broadcast_to(unscale, (16, 2, SLOTS)).reshape(1, 2 * L)
    row_scale = table_weights(quad_weights) * (NPHI ** (-0.5))
    waves = wave_rows(source.reshape(2 * L, 1), jnp.asarray(canonical_table()))
    same, near, far = gathered_table(legendre, magnetic, waves, row_scale, lane_scale)
    slope = radial_slope(magnetic, far, near)
    spec = jnp.concatenate([velocity, magnetic, slope, jnp.zeros_like(velocity)], 0)
    grid = synthesis(offsets, lengths, spec, same, near, far)
    grid = lax.all_to_all(grid, SWAP, 0, 0)
    harmonic = azimuth(grid, waves, row_scale, lane_scale)
    spectra = lax.all_to_all(harmonic, SWAP, 0, 0)
    motional, advected = analysis(offsets, lengths, spectra, same, near, far)
    return motional.reshape(6, 1, PACK), advected.reshape(6, 1, PACK)


def solution(mesh):
    fine = Mesh(mesh.devices.reshape(2, 8, 2, 8, 2), RAD + ORD)
    return jax.shard_map(
        shards,
        mesh=fine,
        in_specs=(
            P(None, RAD, ORD),
            P(None, RAD, ORD),
            P(RAD, ORD),
            P(),
            P(),
            P(ORD),
        ),
        out_specs=(P(None, RAD, ORD), P(None, RAD, ORD)),
        check_vma=False,
    )
```
